256 devices in a mesh: ctx: 32 (over y_lo, z, core), exp: 8 (over y_hi, x).
Axes of the slice: x: 4, y: 4 (y_hi: 2, y_lo: 2; y = y_hi * 2 + y_lo), z: 8, core: 2. Of those that a mesh axis runs over, the one named last changes fastest.
Arguments:
- hidden_in: bfloat16 [4096, 4096], P('ctx', 'exp'), may hold values from -40 to 40
- queries: bfloat16 [4096, 4096], P('ctx', 'exp'), may hold values from -9 to 9
- keys: bfloat16 [4096, 1024], P('ctx', 'exp'), may hold values from -5 to 5
- values: bfloat16 [4096, 1024], P('ctx', 'exp'), may hold values from -9 to 9
- doc_ids: int32 [4096], P('ctx'), may hold values from 0 to 7, never falling along the last dimension, each value on 1 to 3072 neighbouring positions
- out_proj: bfloat16 [4096, 4096], P('exp', 'ctx'), may hold values from -0.375 to 0.375
- norm_gain: float32 [4096], P('exp'), may hold values from 0.1 to 1.9
- routes: int32 [4096, 2], P('ctx'), may hold values from 0 to 7, all different within a row; in each aligned block of 128 rows (0 to 127, 128 to 255, ...) at most 36 rows name the same one
- route_weights: float32 [4096, 2], P('ctx'), may hold values from 0.1 to 0.9
- w_gate: bfloat16 [8, 4096, 14336], P('exp', None, 'ctx'), may hold values from -0.09375 to 0.09375
- w_up: bfloat16 [8, 4096, 14336], P('exp', None, 'ctx'), may hold values from -0.09375 to 0.09375
- w_down: bfloat16 [8, 14336, 4096], P('exp', 'ctx'), may hold values from -0.046875 to 0.046875
Outputs:
- mixed: bfloat16 [4096, 4096], P('ctx', 'exp')
The draws below stay inside these ranges and needn't reach their ends.
Inputs may be any that keep to these rules, and one draw needn't show every extreme that they name: `routes`: within each aligned block of 128 tokens (the tokens of one index of ctx) no expert is named by more than 36 tokens, and in every draw some expert is named by exactly 36 tokens of some block; a token names 2 different experts. `doc_ids`: documents are contiguous and numbered in order; one document is 3072 tokens long.
All inputs are finite; a program needn't handle non-finite values.
Results may differ from the reference program's by a relative error of at most 0.02.
Values may be sent and summed in bfloat16 or wider, within the bound.
No kernel may reach another device: no remote copies, remote signals or barrier semaphores. Data moves between devices by JAX's collectives and lax.ppermute only.
A program may use at most 128 MiB of HBM per device.

```python
import math
import jax
import jax.numpy as jnp
import numpy as np
from jax import lax

D = 4096
HD = 128
FF = 14336
HEADS_DEV = 4
TOP = 2
DOCS = 8
TOK_DEV = 128
KVH = 8
HEADS = 32
EXPERTS = 8
SEQ = 4096
CAP = 36
N_CTX = 32


def draw_keys(key, part):
    key = jax.random.fold_in(key, 7)
    drawn = jnp.clip(1.25 * jax.random.normal(key, (SEQ, KVH * HD)), -5.0, 5.0)
    return drawn.astype(jnp.bfloat16)


def draw_queries(key, part):
    key = jax.random.fold_in(key, 5)
    drawn = jnp.clip(1.25 * jax.random.normal(key, (SEQ, HEADS * HD)), -5.0, 5.0)
    return drawn.astype(jnp.bfloat16)


def draw_hidden_in(key, part):
    key = jax.random.fold_in(key, 3)
    key_a, key_b, key_c = jax.random.split(key, 3)
    column_scale = jnp.exp(jax.random.uniform(key_b, (D,), minval=math.log(0.3), maxval=math.log(3.0)))
    row_scale = jnp.exp(jax.random.uniform(key_c, (SEQ,), minval=math.log(0.3), maxval=math.log(3.0)))
    column_frac = jnp.arange(D, dtype=jnp.float32) / (D - 1)
    column_ramp = 0.6 + 1.2 * column_frac
    noise = jnp.clip(jax.random.normal(key_a, (SEQ, D)), -4.0, 4.0)
    drawn = 0.5 * noise * column_scale[None, :] * row_scale[:, None] * column_ramp[None, :]
    return drawn.astype(jnp.bfloat16)


def levels(stream_key, extent, cuts, low, top_value):
    factor_of, own = 1.0, jax.random.fold_in(stream_key, 6)
    for dim, parts in cuts:
        steps = jnp.exp(jax.random.uniform(jax.random.fold_in(own, dim), (parts,), jnp.float32, low / len(cuts), top_value / len(cuts)))
        factor_of = factor_of * jnp.repeat(steps, extent[dim] // parts).reshape([-1 if axis == dim else 1 for axis in range(len(extent))])
    return factor_of


def length_profile(amount, total, most, skew):
    weights = [(1 << 20) // math.isqrt(standing ** skew) + 1 for standing in range(2, amount + 1)]
    spare, holding = total - most - (amount - 1), [1] * (amount - 1)
    while spare > 0:
        candidates = [i for i in range(amount - 1) if holding[i] < most]
        mass, budget = sum([weights[i] for i in candidates]), spare
        for i in candidates:
            more = min(most - holding[i], max(1, budget * weights[i] // mass), spare)
            holding[i] = holding[i] + more
            spare = spare - more
    return np.array([most] + holding)


def ragged_sizes(stream_key, count, total, most, slope):
    if count == 2:
        one = jax.random.randint(stream_key, (), max(1, total - most), min(most, total - 1) + 1)
        return jnp.stack([one, total - one])
    tallies = jnp.asarray(length_profile(count, total, most, slope), jnp.int32)
    couples = (count - 1) // 2
    source_of, receiver = tallies[1:1 + 2 * couples:2], tallies[2:2 + 2 * couples:2]
    room = jnp.minimum(source_of - 1, most - receiver)
    moved = jax.random.randint(jax.random.fold_in(stream_key, 1), (couples,), 0, 1 << 20) % (room + 1)
    tallies = tallies.at[1:1 + 2 * couples:2].set(source_of - moved).at[2:2 + 2 * couples:2].set(receiver + moved)
    return tallies[jax.random.permutation(jax.random.fold_in(stream_key, 2), count)]


def assign_block(own_key, own, number, rows, number_of, top, bound, skew):
    sequence = jax.random.permutation(own_key, number_of)
    heavy_load, ordinary = portions_of(number_of, rows * top, bound, skew, True), portions_of(number_of, rows * top, bound, skew, False)
    places = jnp.arange(number_of)

    def named(lengths, turn):
        used = int((lengths > 0).sum())
        fixed = max(1, used // 4)
        passed = fixed + (places - fixed + turn * (used - fixed)) % max(1, number_of - fixed)
        return jnp.zeros((number_of,), jnp.int32).at[sequence[jnp.where(places < fixed, places, passed)]].set(jnp.asarray(lengths, jnp.int32))

    lengths = jnp.where(number % 4 == 0, named(heavy_load, number // 4), named(ordinary, number - number // 4 - 1))
    mixed = jax.random.permutation(jax.random.fold_in(own, 3), number_of)
    source_of, sink = mixed[0:number_of // 2 * 2:2], mixed[1:number_of // 2 * 2:2]
    slack = jnp.minimum(lengths[source_of] - 1, bound - lengths[sink]) // 2
    slack = jnp.where((source_of == sequence[0]) | (sink == sequence[0]) | (lengths[sink] == 0), 0, jnp.maximum(slack, 0))
    passed = jax.random.randint(jax.random.fold_in(own, 4), (number_of // 2,), 0, 1 << 20) % (slack + 1)
    lengths = lengths.at[source_of].add(-passed).at[sink].add(passed)
    members = jnp.searchsorted(jnp.cumsum(lengths), jnp.arange(rows * top), side="right").astype(jnp.int32)
    listing = members.reshape(top, rows).T
    listing = listing[jax.random.permutation(jax.random.fold_in(own, 1), rows)]
    turn = jax.random.randint(jax.random.fold_in(own, 2), (rows, 1), 0, top)
    return jnp.take_along_axis(listing, (jnp.arange(top)[None, :] + turn) % top, axis=1)


def portions_of(amount, total, bound, slope, full):
    loads = [(1 << 20) // math.isqrt(grade ** slope) + 1 for grade in range(1, amount + 1)]
    largest = bound if full else min(bound, max(-(-total // amount), total * loads[0] // sum(loads)))
    least = 1 if total - largest >= amount - 1 else 0
    given, rest = [largest] + [least] * (amount - 1), total - largest - least * (amount - 1)
    while rest > 0:
        free = [i for i in range(1, amount) if given[i] < largest] or [i for i in range(1, amount) if given[i] < bound]
        pool, remaining = sum([loads[i] for i in free]), rest
        for i in free:
            more = min(bound - given[i], max(1, remaining * loads[i] // pool), rest)
            given[i] = given[i] + more
            rest = rest - more
    return np.array(given)


def normal_values(key, shape, spread, reach, cuts=(), kind=jnp.bfloat16):
    entries = spread * jax.random.normal(key, shape, jnp.float32)
    if cuts:
        entries = entries * levels(key, shape, cuts, -0.22, 0.18)
    return jnp.clip(entries, -reach, reach).astype(kind)


def setup_inputs(seed: int = 0) -> dict:
    key_of = jax.random.split(jax.random.key(seed), 13)
    hidden_in = draw_hidden_in(jax.random.fold_in(key_of[12], 71), 0)
    queries = draw_queries(jax.random.fold_in(key_of[12], 71), 0)
    keys = draw_keys(jax.random.fold_in(key_of[12], 71), 0)
    values = normal_values(key_of[3], (SEQ, KVH * HD), 1.5, 9.0, ((0, 32), (1, 8)))
    doc_ids = jnp.searchsorted(jnp.cumsum(ragged_sizes(key_of[4], DOCS, SEQ, SEQ * 3 // 4, 2)), jnp.arange(SEQ), side="right").astype(jnp.int32)
    out_proj = normal_values(key_of[5], (HEADS * HD, D), (2 * HD) ** -0.5, 0.375, ((0, 8), (1, 32)))
    norm_gain = jnp.clip(1.0 + 0.18 * jax.random.normal(key_of[6], (D,), jnp.float32), 0.1, 1.9)
    routes_keys = jax.random.split(jax.random.fold_in(key_of[7], 1), SEQ // TOK_DEV)
    routes_turns = jax.random.permutation(jax.random.fold_in(key_of[7], 3), SEQ // TOK_DEV)
    routes = jax.vmap(lambda own, number: assign_block(jax.random.fold_in(key_of[7], 2), own, number, TOK_DEV, EXPERTS, TOP, CAP, 2))(routes_keys, routes_turns).reshape((SEQ, TOP))
    route_weights = jnp.clip(0.1 + 0.79999997 * jax.random.uniform(key_of[8], (SEQ, TOP), jnp.float32) ** levels(key_of[8], (SEQ, TOP), ((0, 32),), -0.2, 0.2), 0.1, 0.9)
    w_gate = normal_values(key_of[9], (EXPERTS, D, FF), D ** -0.5, 0.09375, ((0, 8), (2, 32)))
    w_up = normal_values(key_of[10], (EXPERTS, D, FF), D ** -0.5, 0.09375, ((0, 8), (2, 32)))
    w_down = normal_values(key_of[11], (EXPERTS, FF, D), FF ** -0.5, 0.046875, ((0, 8), (1, 32)))
    return dict(hidden_in=hidden_in, queries=queries, keys=keys, values=values, doc_ids=doc_ids, out_proj=out_proj, norm_gain=norm_gain, routes=routes, route_weights=route_weights, w_gate=w_gate, w_up=w_up, w_down=w_down)


def attend_group(query_group, key_head, value_head, positions, doc_ids):
    score_scale = 1.0 / math.sqrt(HD)
    scores = jnp.einsum('gqd,kd->gqk', query_group.astype(jnp.float32), key_head.astype(jnp.float32)) * score_scale
    visible = (positions[None, :] <= positions[:, None]) & (doc_ids[None, :] == doc_ids[:, None])
    scores = jnp.where(visible[None], scores, -jnp.inf)
    row_max = lax.optimization_barrier(jnp.max(scores, axis=-1, keepdims=True))
    weights = jnp.where(visible[None], jnp.exp(scores - row_max), 0.0)
    weight_sum = lax.optimization_barrier(jnp.sum(weights, axis=-1))
    rounded = lax.optimization_barrier(weights.astype(jnp.bfloat16)).astype(jnp.float32)
    weighted = jnp.einsum('gqk,kd->gqd', rounded, value_head.astype(jnp.float32))
    return (weighted / weight_sum[..., None]).astype(jnp.bfloat16)

def run_expert(operands):
    expert_in, gate_w, up_w, down_w = operands
    gate_part = jnp.dot(expert_in, gate_w, preferred_element_type=jnp.float32)
    up_part = jnp.dot(expert_in, up_w, preferred_element_type=jnp.float32)
    activations = (jax.nn.silu(gate_part) * up_part).astype(jnp.bfloat16)
    block_width = FF // N_CTX

    def add_block(running, block_index):
        act_block = lax.dynamic_slice_in_dim(activations, block_index * block_width, block_width, 1)
        down_block = lax.dynamic_slice_in_dim(down_w, block_index * block_width, block_width, 0)
        partial_value = jnp.dot(act_block, down_block, preferred_element_type=jnp.float32)
        partial_value = lax.optimization_barrier(partial_value.astype(jnp.bfloat16)).astype(jnp.float32)
        return (running + partial_value, None)
    start_sum = jnp.zeros((expert_in.shape[0], D), jnp.float32)
    summed, _ = lax.scan(add_block, start_sum, jnp.arange(N_CTX, dtype=jnp.int32))
    return summed.astype(jnp.bfloat16)

def reference(hidden_in, queries, keys, values, doc_ids, out_proj, norm_gain, routes, route_weights, w_gate, w_up, w_down):
    positions = jnp.arange(SEQ, dtype=jnp.int32)
    query_all = queries.reshape(SEQ, KVH, HEADS_DEV, HD).transpose(1, 2, 0, 3)
    key_all = keys.reshape(SEQ, KVH, HD).transpose(1, 0, 2)
    value_all = values.reshape(SEQ, KVH, HD).transpose(1, 0, 2)
    heads_out = lax.map(lambda group: attend_group(group[0], group[1], group[2], positions, doc_ids), (query_all, key_all, value_all))
    heads_out = heads_out.transpose(2, 0, 1, 3).reshape(SEQ, HEADS * HD)
    projected = jnp.dot(heads_out, out_proj, preferred_element_type=jnp.float32)
    resid = (hidden_in.astype(jnp.float32) + projected).astype(jnp.bfloat16)
    widened = resid.astype(jnp.float32)
    mean_square = lax.optimization_barrier(jnp.mean(widened * widened, axis=1))
    normed = (widened * lax.rsqrt(mean_square + 1e-05)[:, None] * norm_gain[None, :]).astype(jnp.bfloat16)
    expert_ids = jnp.arange(EXPERTS, dtype=jnp.int32)
    hit_counts = lax.optimization_barrier(jnp.sum((routes[:, :, None] == expert_ids).astype(jnp.int32), axis=1))
    slot_rank = jnp.cumsum(hit_counts.reshape(N_CTX, TOK_DEV, EXPERTS), axis=1, dtype=jnp.int32) - 1
    slot_rank = slot_rank.reshape(SEQ, EXPERTS)
    shard_index = positions // TOK_DEV
    slot_index = shard_index[:, None] * CAP + jnp.take_along_axis(slot_rank, routes, axis=1)
    spread_rows = jnp.broadcast_to(normed[:, None, :], (SEQ, TOP, D))
    expert_in = jnp.zeros((EXPERTS, N_CTX * CAP, D), jnp.bfloat16).at[routes, slot_index].set(spread_rows)
    expert_out = lax.map(run_expert, (expert_in, w_gate, w_up, w_down))
    picked = expert_out[routes, slot_index].astype(jnp.float32)
    expert_mix = lax.optimization_barrier(jnp.sum(picked * route_weights[:, :, None], axis=1))
    return (resid.astype(jnp.float32) + expert_mix).astype(jnp.bfloat16)
```

```python
import functools
import math

import jax
import jax.numpy as jnp
from jax import lax
from jax.experimental import pallas as pl
from jax.experimental.pallas import tpu as pltpu
from jax.sharding import PartitionSpec as P

HD = 128
TOP = 2
NORM_EPS = 1e-05
NY, NZ, NK = 2, 8, 2
GROUPS = ((0, 1), (2, 3), (4, 5), (6, 7))
FF_BLOCK = 224


def place(y, z, k):
    return (y % NY) * NZ * NK + (z % NZ) * NK + k


def moves(target):
    return [
        (place(y, z, k), place(*target(y, z, k)))
        for y in range(NY)
        for z in range(NZ)
        for k in range(NK)
    ]


CORE_SWAP = moves(lambda y, z, k: (y, z, 1 - k))
PAIR_SWAP = moves(lambda y, z, k: (1 - y, z, k))
CROSS_SWAP = moves(lambda y, z, k: (1 - y, z, 1 - k))
RING = moves(lambda y, z, k: (y, z + 1 - 2 * k, k))
ENTER = moves(lambda y, z, k: (y, z, 0) if k else (1 - y, z, 1))
LEAVE = moves(lambda y, z, k: (1 - y, z, 0) if k else (y, z, 1))


def send(array, pairs):
    return lax.ppermute(array, "ctx", pairs)


def share_chunk(own, y, k, join):
    core, pair, cross = send(own, CORE_SWAP), send(own, PAIR_SWAP), send(own, CROSS_SWAP)
    here = (jnp.where(k == 0, own, core), jnp.where(k == 0, core, own))
    there = (jnp.where(k == 0, pair, cross), jnp.where(k == 0, cross, pair))
    rows = [jnp.where(y == 0, a, b) for a, b in zip(here + there, there + here)]
    return join(rows)


def ring_gather(chunk, z, k):
    sign = 2 * k - 1
    found = [(chunk, z)]
    moving = chunk
    for step in range(1, NZ // 2 + 1):
        moving = send(moving, RING)
        found.append((moving, (z + sign * step) % NZ))
        if step < NZ // 2:
            found.append((send(moving, CORE_SWAP), (z - sign * step) % NZ))
    return found


def expert_kernel(
    parts, x_ref, g0, u0, d0, g1, u1, d1, *rest
):
    outs, (g_buf, u_buf, d_buf, sems) = rest[:parts], rest[parts:]
    rows = x_ref.shape[0] // parts
    block = g_buf.shape[1]
    blocks = [
        (trio, first)
        for trio in ((g0, u0, d0), (g1, u1, d1))
        for first in range(0, g0.shape[0], block)
    ]
    buffers = (g_buf, u_buf, d_buf)

    def fetch(i, which):
        trio, first = blocks[i]
        return pltpu.make_async_copy(
            trio[which].at[pl.ds(first, block), :],
            buffers[which].at[i % 2],
            sems.at[which, i % 2],
        )

    for which in range(3):
        fetch(0, which).start()
    x = x_ref[...]
    nt = (((1,), (1,)), ((), ()))
    for i in range(len(blocks)):
        if i + 1 < len(blocks):
            for which in range(3):
                fetch(i + 1, which).start()
        fetch(i, 0).wait()
        gate = lax.dot_general(x, g_buf[i % 2], nt, preferred_element_type=jnp.float32)
        fetch(i, 1).wait()
        up = lax.dot_general(x, u_buf[i % 2], nt, preferred_element_type=jnp.float32)
        act = (gate / (1.0 + jnp.exp(-gate)) * up).astype(jnp.bfloat16)
        fetch(i, 2).wait()
        down = jnp.dot(act, d_buf[i % 2], preferred_element_type=jnp.float32)
        for part, out in enumerate(outs):
            piece = down[part * rows : (part + 1) * rows]
            if i == 0:
                out[...] = piece
            else:
                out[...] += piece


def expert_partial(chunks, weights):
    parts = len(chunks)
    x = jnp.concatenate(chunks, axis=0) if parts > 1 else chunks[0]
    rows, width = chunks[0].shape
    hidden = weights[0].shape[0]
    return pl.pallas_call(
        functools.partial(expert_kernel, parts),
        out_shape=[jax.ShapeDtypeStruct((rows, width), jnp.float32)] * parts,
        in_specs=[pl.BlockSpec(memory_space=pltpu.VMEM)]
        + [pl.BlockSpec(memory_space=pl.ANY)] * 6,
        out_specs=[pl.BlockSpec(memory_space=pltpu.VMEM)] * parts,
        scratch_shapes=[pltpu.VMEM((2, FF_BLOCK, width), jnp.bfloat16)] * 3
        + [pltpu.SemaphoreType.DMA((3, 2))],
        compiler_params=pltpu.CompilerParams(vmem_limit_bytes=40 << 20),
        cost_estimate=pl.CostEstimate(
            flops=12 * parts * rows * width * hidden,
            bytes_accessed=12 * width * hidden,
            transcendentals=2 * parts * rows * hidden,
        ),
    )(x, *weights)


def per_device(
    hidden_in,
    queries,
    keys,
    values,
    doc_ids,
    out_proj,
    norm_gain,
    routes,
    route_weights,
    w_gate,
    w_up,
    w_down,
):
    tok_rows, slice_width = hidden_in.shape
    head_count = queries.shape[1] // HD
    experts = lax.axis_size("exp")
    width = slice_width * experts
    ctx_index = lax.axis_index("ctx")
    y, z, k = ctx_index // (NZ * NK), (ctx_index // NK) % NZ, ctx_index % NK
    capacity = min(tok_rows, tok_rows * TOP * 9 // (8 * experts))
    score_scale = 1.0 / math.sqrt(HD)

    doc_rows = jnp.broadcast_to(
        jnp.concatenate([doc_ids, doc_ids])[None, :].astype(jnp.bfloat16), (16, 2 * HD)
    )
    payload = jnp.concatenate([jnp.concatenate([keys, values], axis=1), doc_rows], axis=0)
    kv_found = ring_gather(share_chunk(payload, y, k, jnp.stack), z, k)
    kv = jnp.stack([chunk for chunk, _ in kv_found])
    key_z = jnp.stack([origin for _, origin in kv_found])
    key_all = kv[:, :, :tok_rows, :HD].reshape(-1, HD)
    value_all = kv[:, :, :tok_rows, HD:].reshape(-1, HD)
    key_doc = kv[:, :, tok_rows, :tok_rows].reshape(-1).astype(jnp.int32)
    key_pos = (
        (
            (jnp.arange(4, dtype=jnp.int32) // 2 * NZ * NK + jnp.arange(4, dtype=jnp.int32) % 2)[None, :]
            + key_z[:, None] * NK
        )[:, :, None]
        * tok_rows
        + jnp.arange(tok_rows, dtype=jnp.int32)
    ).reshape(-1)

    proj_found = ring_gather(
        share_chunk(
            out_proj,
            y,
            k,
            lambda rows: jnp.stack(
                [
                    jnp.concatenate([rows[0], rows[1]], axis=1),
                    jnp.concatenate([rows[2], rows[3]], axis=1),
                ]
            ),
        ),
        z,
        k,
    )
    proj_all = jnp.zeros((NY, NZ, out_proj.shape[0], NK * out_proj.shape[1]), jnp.bfloat16)
    for chunk, origin in proj_found:
        proj_all = lax.dynamic_update_slice(proj_all, chunk[:, None], (0, origin, 0, 0))

    own_weights = (
        jnp.swapaxes(w_gate[0], 0, 1),
        jnp.swapaxes(w_up[0], 0, 1),
        w_down[0],
    )
    weights = own_weights + tuple(send(w, CORE_SWAP) for w in own_weights)
    gain = lax.all_gather(norm_gain, "exp", axis=0, tiled=True)

    query_rows = (
        queries.reshape(tok_rows, head_count, HD)
        .transpose(1, 0, 2)
        .reshape(head_count * tok_rows, HD)
    )
    query_pos = jnp.tile(
        ctx_index * tok_rows + jnp.arange(tok_rows, dtype=jnp.int32), head_count
    )
    query_doc = jnp.tile(doc_ids, head_count)
    scores = (
        jnp.einsum("qd,kd->qk", query_rows, key_all, preferred_element_type=jnp.float32)
        * score_scale
    )
    visible = (key_pos[None, :] <= query_pos[:, None]) & (
        key_doc[None, :] == query_doc[:, None]
    )
    scores = jnp.where(visible, scores, -1e30)
    row_max = jnp.max(scores, axis=1)
    soft = jnp.where(visible, jnp.exp(scores - row_max[:, None]), 0.0)
    soft_sum = jnp.sum(soft, axis=1)
    weighted = jnp.dot(soft.astype(jnp.bfloat16), value_all, preferred_element_type=jnp.float32)
    heads_out = (weighted / soft_sum[:, None]).astype(jnp.bfloat16)
    heads_out = (
        heads_out.reshape(head_count, tok_rows, HD)
        .transpose(1, 0, 2)
        .reshape(tok_rows, head_count * HD)
    )

    part = jnp.einsum(
        "td,yzdf->yztf", heads_out, proj_all, preferred_element_type=jnp.float32
    ).astype(jnp.bfloat16)
    part = part.reshape(experts, NY * NZ // experts * tok_rows, -1)
    got = lax.all_to_all(part, "exp", 0, 0, tiled=True)
    summed = jnp.sum(got.astype(jnp.float32), axis=0).reshape(-1, tok_rows, got.shape[2])
    attn_slice = jnp.concatenate([summed[i] for i in range(summed.shape[0])], axis=1)
    resid = (hidden_in.astype(jnp.float32) + attn_slice).astype(jnp.bfloat16)

    expert_ids = jnp.arange(experts, dtype=jnp.int32)
    matches = routes[:, :, None] == expert_ids
    hit_counts = jnp.sum(matches.astype(jnp.int32), axis=1)
    slot_rank = jnp.cumsum(hit_counts, axis=0, dtype=jnp.int32) - 1
    slot_ids = jnp.arange(capacity, dtype=jnp.int32)
    placed_slots = (slot_rank[:, :, None] == slot_ids) & (hit_counts[:, :, None] > 0)
    picked = jnp.einsum(
        "tec,td->ecd",
        placed_slots.astype(jnp.bfloat16),
        resid,
        preferred_element_type=jnp.float32,
    ).astype(jnp.bfloat16)
    picked = lax.all_to_all(picked, "exp", 0, 0, tiled=True)
    rows = picked.transpose(1, 0, 2).reshape(capacity, width).astype(jnp.float32)
    mean_square = jnp.sum(rows * rows, axis=1) / width
    rows = (rows * lax.rsqrt(mean_square + NORM_EPS)[:, None] * gain[None, :]).astype(
        jnp.bfloat16
    )

    entered = send(rows, ENTER)
    crossed = send(rows, PAIR_SWAP)
    chunk = jnp.concatenate(
        [jnp.where(k == 0, rows, entered), jnp.where(k == 0, entered, crossed)], axis=0
    )
    chunks = [chunk]
    for _ in range(NZ - 1):
        chunks.append(send(chunks[-1], RING))
    partials = {}
    for group in GROUPS:
        for step, value in zip(group, expert_partial([chunks[s] for s in group], weights)):
            partials[step] = value
    running = partials[1].astype(jnp.bfloat16)
    for step in range(2, NZ):
        running = (send(running, RING).astype(jnp.float32) + partials[step]).astype(jnp.bfloat16)
    total = send(running, RING).astype(jnp.float32) + partials[0]

    leaving = jnp.where(k == 0, total[capacity:], total[:capacity]).astype(jnp.bfloat16)
    left = send(leaving, LEAVE).astype(jnp.float32)
    back = send(total[capacity:].astype(jnp.bfloat16), PAIR_SWAP).astype(jnp.float32)
    own_out = (jnp.where(k == 0, total[:capacity], back) + left).astype(jnp.bfloat16)

    outs = own_out.reshape(capacity, experts, slice_width).transpose(1, 0, 2)
    expert_out = lax.all_to_all(outs, "exp", 0, 0, tiled=True)
    weight_map = jnp.sum(jnp.where(matches, route_weights[:, :, None], 0.0), axis=1)
    combine = (weight_map[:, :, None] * placed_slots.astype(jnp.float32)).reshape(
        tok_rows, experts * capacity
    )
    expert_flat = expert_out.reshape(experts * capacity, slice_width).astype(jnp.float32)
    expert_mix = jnp.dot(combine, expert_flat, precision=lax.Precision.HIGHEST)
    return (resid.astype(jnp.float32) + expert_mix).astype(jnp.bfloat16)


def solution(mesh):
    in_specs = (
        P("ctx", "exp"),
        P("ctx", "exp"),
        P("ctx", "exp"),
        P("ctx", "exp"),
        P("ctx"),
        P("exp", "ctx"),
        P("exp"),
        P("ctx", None),
        P("ctx", None),
        P("exp", None, "ctx"),
        P("exp", None, "ctx"),
        P("exp", "ctx", None),
    )
    out_specs = P("ctx", "exp")
    return jax.shard_map(
        per_device, mesh=mesh, in_specs=in_specs, out_specs=out_specs, check_vma=False
    )
```

```python
import functools
import math

import jax
import jax.numpy as jnp
from jax import lax
from jax.experimental import pallas as pl
from jax.experimental.pallas import tpu as pltpu
from jax.sharding import PartitionSpec as P

HD = 128
TOP = 2
NORM_EPS = 1e-05
NY, NZ, NK = 2, 8, 2
EXPERT_VMEM = 10 << 20
ATTEND_COST = (8 << 20, 8 << 20)


def place(y, z, k):
    return (y % NY) * NZ * NK + (z % NZ) * NK + k


def moves(target):
    return [
        (place(y, z, k), place(*target(y, z, k)))
        for y in range(NY)
        for z in range(NZ)
        for k in range(NK)
    ]


CORE_SWAP = moves(lambda y, z, k: (y, z, 1 - k))
PAIR_SWAP = moves(lambda y, z, k: (1 - y, z, k))
CROSS_SWAP = moves(lambda y, z, k: (1 - y, z, 1 - k))
RING = moves(lambda y, z, k: (y, z + 1 - 2 * k, k))
ENTER = moves(lambda y, z, k: (y, z, 0) if k else (1 - y, z, 1))
ENTER_SECOND = [(place(y, z, 1), place(y + 1, z, 1)) for y in range(NY) for z in range(NZ)]
LEAVE = moves(lambda y, z, k: (1 - y, z, 0) if k else (y, z, 1))


def send(array, pairs):
    return lax.ppermute(array, "ctx", pairs)


def together(*arrays):
    return lax.optimization_barrier(arrays)


def share(own):
    return [send(own, CORE_SWAP), send(own, PAIR_SWAP), send(own, CROSS_SWAP)]


def in_order(own, shared, y, k):
    core, pair, cross = shared
    here = (jnp.where(k == 0, own, core), jnp.where(k == 0, core, own))
    there = (jnp.where(k == 0, pair, cross), jnp.where(k == 0, cross, pair))
    return [jnp.where(y == 0, a, b) for a, b in zip(here + there, there + here)]


def expert_kernel(x_ref, g0, u0, d0, g1, u1, d1, out_ref):
    x = x_ref[...]
    nt = (((1,), (1,)), ((), ()))
    halves = []
    for gate_ref, up_ref, down_ref in ((g0, u0, d0), (g1, u1, d1)):
        gate = lax.dot_general(x, gate_ref[...], nt, preferred_element_type=jnp.float32)
        up = lax.dot_general(x, up_ref[...], nt, preferred_element_type=jnp.float32)
        act = (gate / (1.0 + jnp.exp(-gate)) * up).astype(jnp.bfloat16)
        halves.append(jnp.dot(act, down_ref[...], preferred_element_type=jnp.float32))
    out_ref[...] = halves[0] + halves[1]


def expert_partial(x, weights):
    rows, width = x.shape
    hidden = weights[0].shape[0]
    return pl.pallas_call(
        expert_kernel,
        out_shape=jax.ShapeDtypeStruct((rows, width), jnp.float32),
        in_specs=[pl.BlockSpec(memory_space=pltpu.VMEM)] * 7,
        out_specs=pl.BlockSpec(memory_space=pltpu.VMEM),
        compiler_params=pltpu.CompilerParams(vmem_limit_bytes=EXPERT_VMEM),
        cost_estimate=pl.CostEstimate(
            flops=12 * rows * width * hidden,
            bytes_accessed=12 * width * hidden,
            transcendentals=2 * rows * hidden,
        ),
    )(x, *weights)


def load_kernel(src_ref, dst_ref, sem):
    copy = pltpu.make_async_copy(src_ref, dst_ref, sem)
    copy.start()
    copy.wait()


def load(array):
    return pl.pallas_call(
        load_kernel,
        out_shape=pltpu.VMEM(array.shape, array.dtype),
        in_specs=[pl.BlockSpec(memory_space=pl.ANY)],
        out_specs=pl.BlockSpec(memory_space=pltpu.VMEM),
        scratch_shapes=[pltpu.SemaphoreType.DMA],
        compiler_params=pltpu.CompilerParams(vmem_limit_bytes=6 << 20),
        cost_estimate=pl.CostEstimate(
            flops=0, bytes_accessed=2 * array.size, transcendentals=0
        ),
    )(array)


def attend_kernel(first, last, parts, info_ref, q_ref, doc_ref, *rest):
    kv_homes, rest = rest[:parts], rest[parts:]
    rest, (kv_refs, sems) = rest[:-2], rest[-2:]
    fetches = [
        pltpu.make_async_copy(home.at[pl.ds(0, kv_refs.shape[1])], kv_refs.at[i], sems.at[i])
        for i, home in enumerate(kv_homes)
    ]
    for fetch in fetches:
        fetch.start()
    ins, outs = (None, rest) if first else (rest[:3], rest[3:])
    toks = q_ref.shape[0]
    heads = q_ref.shape[1] // HD
    shard_rows = toks + 16
    shards = kv_refs.shape[1] // shard_rows
    lane = lax.broadcasted_iota(jnp.int32, (1, toks), 1)
    q_pos = info_ref[0] * toks + lax.broadcasted_iota(jnp.int32, (toks, 1), 0)
    own_doc = doc_ref[:, :1]
    scale = 1.0 / math.sqrt(HD)
    q_all = jnp.concatenate([q_ref[:, h * HD : (h + 1) * HD] for h in range(heads)], axis=0)
    top = total = mixed = None
    if not first:
        top, total, mixed = ins[0][:, :1], ins[1][:, :1], ins[2][...]
    for part, fetch in enumerate(fetches):
        fetch.wait()
        kv_ref = kv_refs.at[part]
        starts = [j * shard_rows for j in range(shards)]
        k_all = jnp.concatenate([kv_ref[j : j + toks, :HD] for j in starts], axis=0)
        v_all = jnp.concatenate([kv_ref[j : j + toks, HD:] for j in starts], axis=0)
        pos = jnp.concatenate(
            [
                ((j // NK) * NZ * NK + info_ref[1 + part] * NK + j % NK) * toks + lane
                for j in range(shards)
            ],
            axis=1,
        )
        doc = jnp.concatenate(
            [kv_ref[j + toks : j + shard_rows, :toks][:1] for j in starts], axis=1
        ).astype(jnp.float32)
        hide = jnp.where((pos <= q_pos) & (doc == own_doc), 0.0, -1e30)
        scores = lax.dot_general(
            q_all, k_all, (((1,), (1,)), ((), ())), preferred_element_type=jnp.float32
        )
        scores = scores * scale + jnp.concatenate([hide] * heads, axis=0)
        new_top = jnp.max(scores, axis=1, keepdims=True)
        if top is not None:
            new_top = jnp.maximum(new_top, top)
        soft = jnp.exp(scores - new_top)
        new_total = jnp.sum(soft, axis=1, keepdims=True)
        new_mixed = jnp.dot(
            soft.astype(jnp.bfloat16), v_all, preferred_element_type=jnp.float32
        )
        if top is not None:
            fade = jnp.exp(top - new_top)
            new_total = new_total + total * fade
            new_mixed = new_mixed + mixed * fade
        top, total, mixed = new_top, new_total, new_mixed
    if last:
        result = (mixed / total).astype(jnp.bfloat16)
        for h in range(heads):
            outs[0][:, h * HD : (h + 1) * HD] = result[h * toks : (h + 1) * toks]
    else:
        outs[0][...] = jnp.broadcast_to(top, (heads * toks, HD))
        outs[1][...] = jnp.broadcast_to(total, (heads * toks, HD))
        outs[2][...] = mixed


def attend(index, queries, doc_cols, state, last, chunks, origins):
    first = state is None
    info = jnp.stack([index, *origins])
    toks, width = queries.shape
    if last:
        out_shape = [jax.ShapeDtypeStruct(queries.shape, jnp.bfloat16)]
    else:
        out_shape = [jax.ShapeDtypeStruct((toks * width // HD, HD), jnp.float32)] * 3
    vmem = pl.BlockSpec(memory_space=pltpu.VMEM)
    after = () if first else tuple(state)
    return pl.pallas_call(
        functools.partial(attend_kernel, first, last, len(chunks)),
        out_shape=out_shape,
        in_specs=[pl.BlockSpec(memory_space=pltpu.SMEM), vmem, vmem]
        + [pl.BlockSpec(memory_space=pl.ANY)] * len(chunks)
        + [vmem] * len(after),
        out_specs=[vmem] * len(out_shape),
        scratch_shapes=[
            pltpu.VMEM((len(chunks), NY * NK * (toks + 16), 2 * HD), chunks[0].dtype),
            pltpu.SemaphoreType.DMA((len(chunks),)),
        ],
        compiler_params=pltpu.CompilerParams(vmem_limit_bytes=16 << 20),
        cost_estimate=pl.CostEstimate(
            flops=0, bytes_accessed=ATTEND_COST[last], transcendentals=0
        ),
    )(info, queries, doc_cols, *chunks, *after)


def swap_blocks(blocks):
    return lax.all_to_all(blocks, "exp", 0, 0, tiled=True)


def norm_kernel(capacity, blocks_ref, out_ref):
    cols = blocks_ref.shape[2]
    rows = [blocks_ref[i].astype(jnp.float32) for i in range(blocks_ref.shape[0])]
    square = sum(
        jnp.sum(r[:capacity] * r[:capacity], axis=1, keepdims=True) for r in rows
    )
    inverse = lax.rsqrt(square / out_ref.shape[1] + NORM_EPS)
    for i, r in enumerate(rows):
        gain = r[capacity : capacity + 1] + (
            r[capacity + 1 : capacity + 2] + r[capacity + 2 : capacity + 3]
        )
        out_ref[:, i * cols : (i + 1) * cols] = (
            r[:capacity] * inverse * gain
        ).astype(jnp.bfloat16)


def normalise(blocks, capacity):
    vmem = pl.BlockSpec(memory_space=pltpu.VMEM)
    count, _, cols = blocks.shape
    return pl.pallas_call(
        functools.partial(norm_kernel, capacity),
        out_shape=jax.ShapeDtypeStruct((capacity, cols * count), jnp.bfloat16),
        in_specs=[vmem],
        out_specs=vmem,
        compiler_params=pltpu.CompilerParams(vmem_limit_bytes=8 << 20),
    )(blocks)


def finish_kernel(core_ref, total_ref, left_ref, back_ref, out_ref):
    count, capacity, cols = out_ref.shape
    whole = jnp.where(
        core_ref[0] == 0, total_ref[:capacity], back_ref[...].astype(jnp.float32)
    ) + left_ref[...].astype(jnp.float32)
    for i in range(count):
        out_ref[i] = whole[:, i * cols : (i + 1) * cols].astype(jnp.bfloat16)


def finish(core, total, left, back, count):
    vmem = pl.BlockSpec(memory_space=pltpu.VMEM)
    capacity, width = left.shape
    return pl.pallas_call(
        finish_kernel,
        out_shape=jax.ShapeDtypeStruct((count, capacity, width // count), jnp.bfloat16),
        in_specs=[pl.BlockSpec(memory_space=pltpu.SMEM)] + [vmem] * 3,
        out_specs=vmem,
        compiler_params=pltpu.CompilerParams(vmem_limit_bytes=8 << 20),
    )(core[None], total, left, back)


def project_kernel(place_ref, heads_ref, *rest):
    blocks, out_ref = rest[:-1], rest[-1]
    heads = heads_ref[...]
    depth = heads.shape[1]
    for i, block in enumerate(blocks):
        rows = slice(block.shape[0] - depth, block.shape[0])
        out_ref[place_ref[i]] = jnp.dot(
            heads, block[rows, :], preferred_element_type=jnp.float32
        ).astype(jnp.bfloat16)


def project(heads_out, found):
    toks, depth = heads_out.shape
    cols = found[0][0].shape[1]
    vmem = pl.BlockSpec(memory_space=pltpu.VMEM)
    return pl.pallas_call(
        project_kernel,
        out_shape=jax.ShapeDtypeStruct((NY * NZ, toks, cols), jnp.bfloat16),
        in_specs=[pl.BlockSpec(memory_space=pltpu.SMEM)] + [vmem] * (1 + len(found)),
        out_specs=vmem,
        compiler_params=pltpu.CompilerParams(vmem_limit_bytes=16 << 20),
        cost_estimate=pl.CostEstimate(
            flops=2 * toks * depth * cols * NY * NZ, bytes_accessed=5 << 20, transcendentals=0
        ),
    )(
        jnp.stack([place for _, place in found]),
        heads_out,
        *[block for block, _ in found],
    )


def per_device(
    hidden_in,
    queries,
    keys,
    values,
    doc_ids,
    out_proj,
    norm_gain,
    routes,
    route_weights,
    w_gate,
    w_up,
    w_down,
):
    tok_rows, slice_width = hidden_in.shape
    experts = lax.axis_size("exp")
    width = slice_width * experts
    ctx_index = lax.axis_index("ctx")
    y, z, k = ctx_index // (NZ * NK), (ctx_index // NK) % NZ, ctx_index % NK
    capacity = min(tok_rows, tok_rows * TOP * 9 // (8 * experts))

    doc_rows = jnp.broadcast_to(
        jnp.concatenate([doc_ids, doc_ids])[None, :].astype(jnp.bfloat16), (16, 2 * HD)
    )
    payload = jnp.concatenate([jnp.concatenate([keys, values], axis=1), doc_rows], axis=0)
    payload, out_proj = together(payload, out_proj)
    kv_shared = share(payload)
    proj_other = send(out_proj, CORE_SWAP)
    proj_block = jnp.concatenate(
        [jnp.where(k == 0, out_proj, proj_other), jnp.where(k == 0, proj_other, out_proj)],
        axis=1,
    )
    chunk = jnp.concatenate(in_order(payload, kv_shared, y, k) + [proj_block], axis=0)
    depth = out_proj.shape[0]

    own_weights = (
        jnp.swapaxes(w_gate[0], 0, 1),
        jnp.swapaxes(w_up[0], 0, 1),
        w_down[0],
    )
    weights = own_weights + tuple(send(w, CORE_SWAP) for w in own_weights)
    weights = [load(w) for w in weights]

    doc_cols = jnp.broadcast_to(doc_ids[:, None].astype(jnp.float32), (tok_rows, HD))
    visit = functools.partial(attend, ctx_index, queries, doc_cols)
    sign = 2 * k - 1
    hops = NZ // 2
    own_side, other_side = y * NZ, (1 - y) * NZ
    found, chunks, origins = [(chunk, own_side + z)], [chunk], [z]
    across = None
    for step in range(1, hops + 2):
        ahead = (z + sign * (step - 1)) % NZ
        astern = (z - sign * (step - 1)) % NZ
        behind = (z - sign * (step - 2)) % NZ
        sent = [send(chunk[-depth:], PAIR_SWAP)]
        if step <= hops:
            sent.append(send(chunk, RING))
        if 1 < step <= hops:
            sent.append(send(chunk, CORE_SWAP))
        if step > 2:
            sent.append(send(across, CORE_SWAP))
        sent = list(together(*sent))
        across = sent.pop(0)
        found.append((across, other_side + ahead))
        if step > 2:
            found.append((sent.pop(), other_side + behind))
        if 1 < step <= hops:
            swapped = sent.pop()
            found.append((swapped, own_side + astern))
            chunks.append(swapped)
            origins.append(astern)
        if step <= hops:
            chunk = sent.pop()
            ahead = (z + sign * step) % NZ
            found.append((chunk, own_side + ahead))
            chunks.append(chunk)
            origins.append(ahead)
    (heads_out,) = visit(None, True, chunks, origins)

    part = project(heads_out, found)
    part = part.reshape(experts, NY * NZ // experts * tok_rows, -1)
    summed = jnp.sum(swap_blocks(part).astype(jnp.float32), axis=0)
    summed = summed.reshape(-1, tok_rows, summed.shape[1])
    attn_slice = jnp.concatenate([summed[i] for i in range(summed.shape[0])], axis=1)
    resid = (hidden_in.astype(jnp.float32) + attn_slice).astype(jnp.bfloat16)

    expert_ids = jnp.arange(experts, dtype=jnp.int32)
    matches = routes[:, :, None] == expert_ids
    hit_counts = jnp.sum(matches.astype(jnp.int32), axis=1)
    slot_rank = jnp.cumsum(hit_counts, axis=0, dtype=jnp.int32) - 1
    slot_ids = jnp.arange(capacity, dtype=jnp.int32)
    placed_slots = (slot_rank[:, :, None] == slot_ids) & (hit_counts[:, :, None] > 0)
    picked = jnp.einsum(
        "tec,td->ecd",
        placed_slots.astype(jnp.bfloat16),
        resid,
        preferred_element_type=jnp.float32,
    ).astype(jnp.bfloat16)
    high = lax.reduce_precision(norm_gain, 8, 7)
    middle = lax.reduce_precision(norm_gain - high, 8, 7)
    low = norm_gain - high - middle
    gain_rows = jnp.stack([high, middle, low, jnp.zeros_like(low)]).astype(jnp.bfloat16)
    picked = jnp.concatenate(
        [picked, jnp.broadcast_to(gain_rows, (experts, *gain_rows.shape))], axis=1
    )
    rows = normalise(swap_blocks(picked), capacity)

    entered = send(rows, ENTER)
    crossed = send(rows, ENTER_SECOND)
    chunk = jnp.concatenate(
        [jnp.where(k == 0, rows, entered), jnp.where(k == 0, entered, crossed)], axis=0
    )
    chunks = [chunk]
    for _ in range(NZ - 1):
        chunks.append(send(chunks[-1], RING))
    running = None
    for step in range(1, NZ):
        part = expert_partial(chunks[step], weights)
        if step > 1:
            part = send(running, RING).astype(jnp.float32) + part
        running = part.astype(jnp.bfloat16)
    part = expert_partial(chunks[0], weights)
    total = send(running, RING).astype(jnp.float32) + part

    leaving = jnp.where(k == 0, total[capacity:], total[:capacity]).astype(jnp.bfloat16)
    left = send(leaving, LEAVE)
    back = send(total[capacity:].astype(jnp.bfloat16), ENTER_SECOND)

    expert_out = swap_blocks(finish(k, total, left, back, experts))
    weight_map = jnp.sum(jnp.where(matches, route_weights[:, :, None], 0.0), axis=1)
    combine = (weight_map[:, :, None] * placed_slots.astype(jnp.float32)).reshape(
        tok_rows, experts * capacity
    )
    expert_flat = expert_out.reshape(experts * capacity, slice_width).astype(jnp.float32)
    expert_mix = jnp.dot(combine, expert_flat, precision=lax.Precision.HIGHEST)
    return (resid.astype(jnp.float32) + expert_mix).astype(jnp.bfloat16)


def solution(mesh):
    in_specs = (
        P("ctx", "exp"),
        P("ctx", "exp"),
        P("ctx", "exp"),
        P("ctx", "exp"),
        P("ctx"),
        P("exp", "ctx"),
        P("exp"),
        P("ctx", None),
        P("ctx", None),
        P("exp", None, "ctx"),
        P("exp", None, "ctx"),
        P("exp", "ctx", None),
    )
    out_specs = P("ctx", "exp")
    return jax.shard_map(
        per_device, mesh=mesh, in_specs=in_specs, out_specs=out_specs, check_vma=False
    )
```

```python
import functools
import math

import jax
import jax.numpy as jnp
from jax import lax
from jax.experimental import pallas as pl
from jax.experimental.pallas import tpu as pltpu
from jax.sharding import PartitionSpec as P

HD = 128
TOP = 2
NORM_EPS = 1e-05
NY, NZ, NK = 2, 8, 2
EXPERT_VMEM = 10 << 20


def place(y, z, k):
    return (y % NY) * NZ * NK + (z % NZ) * NK + k


def moves(target):
    return [
        (place(y, z, k), place(*target(y, z, k)))
        for y in range(NY)
        for z in range(NZ)
        for k in range(NK)
    ]


CORE_SWAP = moves(lambda y, z, k: (y, z, 1 - k))
PAIR_SWAP = moves(lambda y, z, k: (1 - y, z, k))
CROSS_SWAP = moves(lambda y, z, k: (1 - y, z, 1 - k))
RING = moves(lambda y, z, k: (y, z + 1 - 2 * k, k))
ENTER = moves(lambda y, z, k: (y, z, 0) if k else (1 - y, z, 1))
ENTER_SECOND = [(place(y, z, 1), place(y + 1, z, 1)) for y in range(NY) for z in range(NZ)]
LEAVE = moves(lambda y, z, k: (1 - y, z, 0) if k else (y, z, 1))


def send(array, pairs):
    return lax.ppermute(array, "ctx", pairs)


def together(*arrays):
    return lax.optimization_barrier(arrays)


def share(own):
    return [send(own, CORE_SWAP), send(own, PAIR_SWAP), send(own, CROSS_SWAP)]


def in_order(own, shared, y, k):
    core, pair, cross = shared
    here = (jnp.where(k == 0, own, core), jnp.where(k == 0, core, own))
    there = (jnp.where(k == 0, pair, cross), jnp.where(k == 0, cross, pair))
    return [jnp.where(y == 0, a, b) for a, b in zip(here + there, there + here)]


def expert_kernel(x_ref, g0, u0, d0, g1, u1, d1, out_ref):
    x = x_ref[...]
    nt = (((1,), (1,)), ((), ()))
    halves = []
    for gate_ref, up_ref, down_ref in ((g0, u0, d0), (g1, u1, d1)):
        gate = lax.dot_general(x, gate_ref[...], nt, preferred_element_type=jnp.float32)
        up = lax.dot_general(x, up_ref[...], nt, preferred_element_type=jnp.float32)
        act = (gate / (1.0 + jnp.exp(-gate)) * up).astype(jnp.bfloat16)
        halves.append(jnp.dot(act, down_ref[...], preferred_element_type=jnp.float32))
    out_ref[...] = halves[0] + halves[1]


def expert_partial(x, weights):
    rows, width = x.shape
    hidden = weights[0].shape[0]
    return pl.pallas_call(
        expert_kernel,
        out_shape=jax.ShapeDtypeStruct((rows, width), jnp.float32),
        in_specs=[pl.BlockSpec(memory_space=pltpu.VMEM)] * 7,
        out_specs=pl.BlockSpec(memory_space=pltpu.VMEM),
        compiler_params=pltpu.CompilerParams(vmem_limit_bytes=EXPERT_VMEM),
        cost_estimate=pl.CostEstimate(
            flops=12 * rows * width * hidden,
            bytes_accessed=12 * width * hidden,
            transcendentals=2 * rows * hidden,
        ),
    )(x, *weights)


def load_kernel(count, *refs):
    sources, targets, sems = refs[:count], refs[count:-1], refs[-1]
    copies = [
        pltpu.make_async_copy(source, target, sems.at[i])
        for i, (source, target) in enumerate(zip(sources, targets))
    ]
    for copy in copies:
        copy.start()
    for copy in copies:
        copy.wait()


def load(arrays):
    count = len(arrays)
    return pl.pallas_call(
        functools.partial(load_kernel, count),
        out_shape=[pltpu.VMEM(a.shape, a.dtype) for a in arrays],
        in_specs=[pl.BlockSpec(memory_space=pl.ANY)] * count,
        out_specs=[pl.BlockSpec(memory_space=pltpu.VMEM)] * count,
        scratch_shapes=[pltpu.SemaphoreType.DMA((count,))],
        compiler_params=pltpu.CompilerParams(vmem_limit_bytes=6 << 20),
        cost_estimate=pl.CostEstimate(
            flops=0, bytes_accessed=2 * count * arrays[0].size, transcendentals=0
        ),
    )(*arrays)


def attend_kernel(parts, info_ref, q_ref, doc_ref, *rest):
    kv_refs, out_ref = rest[:parts], rest[parts]
    toks = q_ref.shape[0]
    heads = q_ref.shape[1] // HD
    shard_rows = toks + 16
    starts = [j * shard_rows for j in range(NY * NK)]
    lane = lax.broadcasted_iota(jnp.int32, (1, toks), 1)
    q_pos = info_ref[0] * toks + lax.broadcasted_iota(jnp.int32, (toks, 1), 0)
    own_doc = doc_ref[:, :1]
    scale = 1.0 / math.sqrt(HD)
    q_all = jnp.concatenate([q_ref[:, h * HD : (h + 1) * HD] for h in range(heads)], axis=0)
    top = total = mixed = None
    for part, kv_ref in enumerate(kv_refs):
        k_all = jnp.concatenate([kv_ref[j : j + toks, :HD] for j in starts], axis=0)
        v_all = jnp.concatenate([kv_ref[j : j + toks, HD:] for j in starts], axis=0)
        pos = jnp.concatenate(
            [
                ((j // NK) * NZ * NK + info_ref[1 + part] * NK + j % NK) * toks + lane
                for j in range(NY * NK)
            ],
            axis=1,
        )
        doc = jnp.concatenate(
            [kv_ref[j + toks : j + shard_rows, :toks][:1] for j in starts], axis=1
        ).astype(jnp.float32)
        hide = jnp.where((pos <= q_pos) & (doc == own_doc), 0.0, -1e30)
        scores = lax.dot_general(
            q_all, k_all, (((1,), (1,)), ((), ())), preferred_element_type=jnp.float32
        )
        scores = scores * scale + jnp.concatenate([hide] * heads, axis=0)
        new_top = jnp.max(scores, axis=1, keepdims=True)
        if top is not None:
            new_top = jnp.maximum(new_top, top)
        soft = jnp.exp(scores - new_top)
        new_total = jnp.sum(soft, axis=1, keepdims=True)
        new_mixed = jnp.dot(
            soft.astype(jnp.bfloat16), v_all, preferred_element_type=jnp.float32
        )
        if top is not None:
            fade = jnp.exp(top - new_top)
            new_total = new_total + total * fade
            new_mixed = new_mixed + mixed * fade
        top, total, mixed = new_top, new_total, new_mixed
    result = (mixed / total).astype(jnp.bfloat16)
    for h in range(heads):
        out_ref[:, h * HD : (h + 1) * HD] = result[h * toks : (h + 1) * toks]


def attend(index, queries, doc_cols, chunks, origins):
    info = jnp.stack([index, *origins])
    toks, width = queries.shape
    vmem = pl.BlockSpec(memory_space=pltpu.VMEM)
    scored = toks * width // HD * NY * NK * toks * len(chunks)
    return pl.pallas_call(
        functools.partial(attend_kernel, len(chunks)),
        out_shape=jax.ShapeDtypeStruct(queries.shape, jnp.bfloat16),
        in_specs=[pl.BlockSpec(memory_space=pltpu.SMEM)] + [vmem] * (2 + len(chunks)),
        out_specs=vmem,
        compiler_params=pltpu.CompilerParams(vmem_limit_bytes=16 << 20),
        cost_estimate=pl.CostEstimate(
            flops=4 * scored * HD, bytes_accessed=8 << 20, transcendentals=scored
        ),
    )(info, queries, doc_cols, *chunks)


def pin_kernel(x_ref, out_ref):
    out_ref[...] = x_ref[...]


def pin(x):
    return pl.pallas_call(
        pin_kernel,
        out_shape=pltpu.VMEM(x.shape, x.dtype),
        in_specs=[pl.BlockSpec(memory_space=pltpu.VMEM)],
        out_specs=pl.BlockSpec(memory_space=pltpu.VMEM),
        compiler_params=pltpu.CompilerParams(vmem_limit_bytes=4 << 20),
        cost_estimate=pl.CostEstimate(flops=0, bytes_accessed=1 << 10, transcendentals=0),
    )(x)


def swap_blocks(blocks):
    return lax.all_to_all(blocks, "exp", 0, 0, tiled=True)


def norm_kernel(capacity, blocks_ref, out_ref):
    cols = blocks_ref.shape[2]
    rows = [blocks_ref[i].astype(jnp.float32) for i in range(blocks_ref.shape[0])]
    square = sum(
        jnp.sum(r[:capacity] * r[:capacity], axis=1, keepdims=True) for r in rows
    )
    inverse = lax.rsqrt(square / out_ref.shape[1] + NORM_EPS)
    for i, r in enumerate(rows):
        gain = r[capacity : capacity + 1] + (
            r[capacity + 1 : capacity + 2] + r[capacity + 2 : capacity + 3]
        )
        out_ref[:, i * cols : (i + 1) * cols] = (
            r[:capacity] * inverse * gain
        ).astype(jnp.bfloat16)


def normalise(blocks, capacity):
    vmem = pl.BlockSpec(memory_space=pltpu.VMEM)
    count, _, cols = blocks.shape
    return pl.pallas_call(
        functools.partial(norm_kernel, capacity),
        out_shape=jax.ShapeDtypeStruct((capacity, cols * count), jnp.bfloat16),
        in_specs=[vmem],
        out_specs=vmem,
        compiler_params=pltpu.CompilerParams(vmem_limit_bytes=8 << 20),
    )(blocks)


def finish_kernel(core_ref, total_ref, left_ref, back_ref, out_ref):
    count, capacity, cols = out_ref.shape
    whole = jnp.where(
        core_ref[0] == 0, total_ref[:capacity], back_ref[...].astype(jnp.float32)
    ) + left_ref[...].astype(jnp.float32)
    for i in range(count):
        out_ref[i] = whole[:, i * cols : (i + 1) * cols].astype(jnp.bfloat16)


def finish(core, total, left, back, count):
    vmem = pl.BlockSpec(memory_space=pltpu.VMEM)
    capacity, width = left.shape
    return pl.pallas_call(
        finish_kernel,
        out_shape=jax.ShapeDtypeStruct((count, capacity, width // count), jnp.bfloat16),
        in_specs=[pl.BlockSpec(memory_space=pltpu.SMEM)] + [vmem] * 3,
        out_specs=vmem,
        compiler_params=pltpu.CompilerParams(vmem_limit_bytes=8 << 20),
    )(core[None], total, left, back)


def project_kernel(place_ref, heads_ref, *rest):
    blocks, out_ref = rest[:-1], rest[-1]
    heads = heads_ref[...]
    depth = heads.shape[1]
    for i, block in enumerate(blocks):
        rows = slice(block.shape[0] - depth, block.shape[0])
        out_ref[place_ref[i]] = jnp.dot(
            heads, block[rows, :], preferred_element_type=jnp.float32
        ).astype(jnp.bfloat16)


def project(heads_out, found):
    toks, depth = heads_out.shape
    cols = found[0][0].shape[1]
    vmem = pl.BlockSpec(memory_space=pltpu.VMEM)
    return pl.pallas_call(
        project_kernel,
        out_shape=jax.ShapeDtypeStruct((NY * NZ, toks, cols), jnp.bfloat16),
        in_specs=[pl.BlockSpec(memory_space=pltpu.SMEM)] + [vmem] * (1 + len(found)),
        out_specs=vmem,
        compiler_params=pltpu.CompilerParams(vmem_limit_bytes=16 << 20),
        cost_estimate=pl.CostEstimate(
            flops=2 * toks * depth * cols * NY * NZ, bytes_accessed=5 << 20, transcendentals=0
        ),
    )(
        jnp.stack([place for _, place in found]),
        heads_out,
        *[block for block, _ in found],
    )


def per_device(
    hidden_in,
    queries,
    keys,
    values,
    doc_ids,
    out_proj,
    norm_gain,
    routes,
    route_weights,
    w_gate,
    w_up,
    w_down,
):
    tok_rows, slice_width = hidden_in.shape
    experts = lax.axis_size("exp")
    width = slice_width * experts
    ctx_index = lax.axis_index("ctx")
    y, z, k = ctx_index // (NZ * NK), (ctx_index // NK) % NZ, ctx_index % NK
    capacity = min(tok_rows, tok_rows * TOP * 9 // (8 * experts))

    doc_rows = jnp.broadcast_to(
        jnp.concatenate([doc_ids, doc_ids])[None, :].astype(jnp.bfloat16), (16, 2 * HD)
    )
    payload = jnp.concatenate([jnp.concatenate([keys, values], axis=1), doc_rows], axis=0)
    payload, out_proj = together(payload, out_proj)
    kv_shared = share(payload)
    proj_other = send(out_proj, CORE_SWAP)
    proj_block = jnp.concatenate(
        [jnp.where(k == 0, out_proj, proj_other), jnp.where(k == 0, proj_other, out_proj)],
        axis=1,
    )
    chunk = jnp.concatenate(in_order(payload, kv_shared, y, k) + [proj_block], axis=0)
    depth = out_proj.shape[0]

    own_weights = (
        jnp.swapaxes(w_gate[0], 0, 1),
        jnp.swapaxes(w_up[0], 0, 1),
        w_down[0],
    )
    weights = [*load(own_weights), *load([send(w, CORE_SWAP) for w in own_weights])]

    doc_cols = jnp.broadcast_to(doc_ids[:, None].astype(jnp.float32), (tok_rows, HD))
    sign = 2 * k - 1
    hops = NZ // 2
    own_side, other_side = y * NZ, (1 - y) * NZ
    found, chunks, origins = [(chunk, own_side + z)], [chunk], [z]
    across = None
    for step in range(1, hops + 2):
        ahead = (z + sign * (step - 1)) % NZ
        astern = (z - sign * (step - 1)) % NZ
        behind = (z - sign * (step - 2)) % NZ
        sent = [send(chunk[-depth:], PAIR_SWAP)]
        if step <= hops:
            sent.append(send(chunk, RING))
        if 1 < step <= hops:
            sent.append(send(chunk, CORE_SWAP))
        if step > 2:
            sent.append(send(across, CORE_SWAP))
        sent = list(together(*sent))
        across = sent.pop(0)
        found.append((across, other_side + ahead))
        if step > 2:
            found.append((sent.pop(), other_side + behind))
        if 1 < step <= hops:
            swapped = pin(sent.pop())
            found.append((swapped, own_side + astern))
            chunks.append(swapped)
            origins.append(astern)
        if step <= hops:
            chunk = pin(sent.pop())
            ahead = (z + sign * step) % NZ
            found.append((chunk, own_side + ahead))
            chunks.append(chunk)
            origins.append(ahead)
    heads_out = attend(ctx_index, queries, doc_cols, chunks, origins)

    part = project(heads_out, found)
    part = part.reshape(experts, NY * NZ // experts * tok_rows, -1)
    summed = jnp.sum(swap_blocks(part).astype(jnp.float32), axis=0)
    summed = summed.reshape(-1, tok_rows, summed.shape[1])
    attn_slice = jnp.concatenate([summed[i] for i in range(summed.shape[0])], axis=1)
    resid = (hidden_in.astype(jnp.float32) + attn_slice).astype(jnp.bfloat16)

    expert_ids = jnp.arange(experts, dtype=jnp.int32)
    matches = routes[:, :, None] == expert_ids
    hit_counts = jnp.sum(matches.astype(jnp.int32), axis=1)
    slot_rank = jnp.cumsum(hit_counts, axis=0, dtype=jnp.int32) - 1
    slot_ids = jnp.arange(capacity, dtype=jnp.int32)
    placed_slots = (slot_rank[:, :, None] == slot_ids) & (hit_counts[:, :, None] > 0)
    picked = jnp.einsum(
        "tec,td->ecd",
        placed_slots.astype(jnp.bfloat16),
        resid,
        preferred_element_type=jnp.float32,
    ).astype(jnp.bfloat16)
    high = lax.reduce_precision(norm_gain, 8, 7)
    middle = lax.reduce_precision(norm_gain - high, 8, 7)
    low = norm_gain - high - middle
    gain_rows = jnp.stack([high, middle, low, jnp.zeros_like(low)]).astype(jnp.bfloat16)
    picked = jnp.concatenate(
        [picked, jnp.broadcast_to(gain_rows, (experts, *gain_rows.shape))], axis=1
    )
    rows = normalise(swap_blocks(picked), capacity)

    entered = send(rows, ENTER)
    crossed = send(rows, ENTER_SECOND)
    chunk = jnp.concatenate(
        [jnp.where(k == 0, rows, entered), jnp.where(k == 0, entered, crossed)], axis=0
    )
    chunks = [chunk]
    for _ in range(NZ - 1):
        chunks.append(send(chunks[-1], RING))
    running = None
    for step in range(1, NZ):
        part = expert_partial(chunks[step], weights)
        if step > 1:
            part = send(running, RING).astype(jnp.float32) + part
        running = part.astype(jnp.bfloat16)
    part = expert_partial(chunks[0], weights)
    total = send(running, RING).astype(jnp.float32) + part

    leaving = jnp.where(k == 0, total[capacity:], total[:capacity]).astype(jnp.bfloat16)
    left = send(leaving, LEAVE)
    back = send(total[capacity:].astype(jnp.bfloat16), ENTER_SECOND)

    expert_out = swap_blocks(finish(k, total, left, back, experts))
    weight_map = jnp.sum(jnp.where(matches, route_weights[:, :, None], 0.0), axis=1)
    combine = (weight_map[:, :, None] * placed_slots.astype(jnp.float32)).reshape(
        tok_rows, experts * capacity
    )
    expert_flat = expert_out.reshape(experts * capacity, slice_width).astype(jnp.float32)
    expert_mix = jnp.dot(combine, expert_flat, precision=lax.Precision.HIGHEST)
    return (resid.astype(jnp.float32) + expert_mix).astype(jnp.bfloat16)


def solution(mesh):
    in_specs = (
        P("ctx", "exp"),
        P("ctx", "exp"),
        P("ctx", "exp"),
        P("ctx", "exp"),
        P("ctx"),
        P("exp", "ctx"),
        P("exp"),
        P("ctx", None),
        P("ctx", None),
        P("exp", None, "ctx"),
        P("exp", None, "ctx"),
        P("exp", "ctx", None),
    )
    out_specs = P("ctx", "exp")
    return jax.shard_map(
        per_device, mesh=mesh, in_specs=in_specs, out_specs=out_specs, check_vma=False
    )
```

```python
import functools
import math

import jax
import jax.numpy as jnp
from jax import lax
from jax.experimental import pallas as pl
from jax.experimental.pallas import tpu as pltpu
from jax.sharding import PartitionSpec as P

HD = 128
TOP = 2
NORM_EPS = 1e-05
NY, NZ, NK = 2, 8, 2
EXPERT_VMEM = 10 << 20


def place(y, z, k):
    return (y % NY) * NZ * NK + (z % NZ) * NK + k


def moves(target):
    return [
        (place(y, z, k), place(*target(y, z, k)))
        for y in range(NY)
        for z in range(NZ)
        for k in range(NK)
    ]


CORE_SWAP = moves(lambda y, z, k: (y, z, 1 - k))
PAIR_SWAP = moves(lambda y, z, k: (1 - y, z, k))
CROSS_SWAP = moves(lambda y, z, k: (1 - y, z, 1 - k))
RING = moves(lambda y, z, k: (y, z + 1 - 2 * k, k))
ENTER = moves(lambda y, z, k: (y, z, 0) if k else (1 - y, z, 1))
ENTER_SECOND = [(place(y, z, 1), place(y + 1, z, 1)) for y in range(NY) for z in range(NZ)]
LEAVE = moves(lambda y, z, k: (1 - y, z, 0) if k else (y, z, 1))


def send(array, pairs):
    return lax.ppermute(array, "ctx", pairs)


def together(*arrays):
    return lax.optimization_barrier(arrays)


def share(own):
    return [send(own, CORE_SWAP), send(own, PAIR_SWAP), send(own, CROSS_SWAP)]


def in_order(own, shared, y, k):
    core, pair, cross = shared
    here = (jnp.where(k == 0, own, core), jnp.where(k == 0, core, own))
    there = (jnp.where(k == 0, pair, cross), jnp.where(k == 0, cross, pair))
    return [jnp.where(y == 0, a, b) for a, b in zip(here + there, there + here)]


def expert_kernel(x_ref, g0, u0, d0, g1, u1, d1, out_ref):
    x = x_ref[...]
    nt = (((1,), (1,)), ((), ()))
    halves = []
    for gate_ref, up_ref, down_ref in ((g0, u0, d0), (g1, u1, d1)):
        gate = lax.dot_general(x, gate_ref[...], nt, preferred_element_type=jnp.float32)
        up = lax.dot_general(x, up_ref[...], nt, preferred_element_type=jnp.float32)
        act = (gate / (1.0 + jnp.exp(-gate)) * up).astype(jnp.bfloat16)
        halves.append(jnp.dot(act, down_ref[...], preferred_element_type=jnp.float32))
    out_ref[...] = halves[0] + halves[1]


def expert_partial(x, weights):
    rows, width = x.shape
    hidden = weights[0].shape[0]
    return pl.pallas_call(
        expert_kernel,
        out_shape=jax.ShapeDtypeStruct((rows, width), jnp.float32),
        in_specs=[pl.BlockSpec(memory_space=pltpu.VMEM)] * 7,
        out_specs=pl.BlockSpec(memory_space=pltpu.VMEM),
        compiler_params=pltpu.CompilerParams(vmem_limit_bytes=EXPERT_VMEM),
        cost_estimate=pl.CostEstimate(
            flops=12 * rows * width * hidden,
            bytes_accessed=12 * width * hidden,
            transcendentals=2 * rows * hidden,
        ),
    )(x, *weights)


def load_kernel(count, *refs):
    sources, targets, sems = refs[:count], refs[count:-1], refs[-1]
    copies = [
        pltpu.make_async_copy(source, target, sems.at[i])
        for i, (source, target) in enumerate(zip(sources, targets))
    ]
    for copy in copies:
        copy.start()
    for copy in copies:
        copy.wait()


def load(arrays):
    count = len(arrays)
    return pl.pallas_call(
        functools.partial(load_kernel, count),
        out_shape=[pltpu.VMEM(a.shape, a.dtype) for a in arrays],
        in_specs=[pl.BlockSpec(memory_space=pl.ANY)] * count,
        out_specs=[pl.BlockSpec(memory_space=pltpu.VMEM)] * count,
        scratch_shapes=[pltpu.SemaphoreType.DMA((count,))],
        compiler_params=pltpu.CompilerParams(vmem_limit_bytes=6 << 20),
        cost_estimate=pl.CostEstimate(
            flops=0, bytes_accessed=2 * count * arrays[0].size, transcendentals=0
        ),
    )(*arrays)


def attend_kernel(parts, info_ref, q_ref, doc_ref, *rest):
    kv_refs, out_ref = rest[:parts], rest[parts]
    toks = q_ref.shape[0]
    heads = q_ref.shape[1] // HD
    shard_rows = toks + 16
    starts = [j * shard_rows for j in range(NY * NK)]
    lane = lax.broadcasted_iota(jnp.int32, (1, toks), 1)
    q_pos = info_ref[0] * toks + lax.broadcasted_iota(jnp.int32, (toks, 1), 0)
    own_doc = doc_ref[:, :1]
    scale = 1.0 / math.sqrt(HD)
    q_all = jnp.concatenate([q_ref[:, h * HD : (h + 1) * HD] for h in range(heads)], axis=0)
    top = total = mixed = None
    for part, kv_ref in enumerate(kv_refs):
        k_all = jnp.concatenate([kv_ref[j : j + toks, :HD] for j in starts], axis=0)
        v_all = jnp.concatenate([kv_ref[j : j + toks, HD:] for j in starts], axis=0)
        pos = jnp.concatenate(
            [
                ((j // NK) * NZ * NK + info_ref[1 + part] * NK + j % NK) * toks + lane
                for j in range(NY * NK)
            ],
            axis=1,
        )
        doc = jnp.concatenate(
            [kv_ref[j + toks : j + shard_rows, :toks][:1] for j in starts], axis=1
        ).astype(jnp.float32)
        hide = jnp.where((pos <= q_pos) & (doc == own_doc), 0.0, -1e30)
        scores = lax.dot_general(
            q_all, k_all, (((1,), (1,)), ((), ())), preferred_element_type=jnp.float32
        )
        scores = scores * scale + jnp.concatenate([hide] * heads, axis=0)
        new_top = jnp.max(scores, axis=1, keepdims=True)
        if top is not None:
            new_top = jnp.maximum(new_top, top)
        soft = jnp.exp(scores - new_top)
        new_total = jnp.sum(soft, axis=1, keepdims=True)
        new_mixed = jnp.dot(
            soft.astype(jnp.bfloat16), v_all, preferred_element_type=jnp.float32
        )
        if top is not None:
            fade = jnp.exp(top - new_top)
            new_total = new_total + total * fade
            new_mixed = new_mixed + mixed * fade
        top, total, mixed = new_top, new_total, new_mixed
    result = (mixed / total).astype(jnp.bfloat16)
    for h in range(heads):
        out_ref[:, h * HD : (h + 1) * HD] = result[h * toks : (h + 1) * toks]


def attend(index, queries, doc_cols, chunks, origins):
    info = jnp.stack([index, *origins])
    toks, width = queries.shape
    vmem = pl.BlockSpec(memory_space=pltpu.VMEM)
    scored = toks * width // HD * NY * NK * toks * len(chunks)
    return pl.pallas_call(
        functools.partial(attend_kernel, len(chunks)),
        out_shape=jax.ShapeDtypeStruct(queries.shape, jnp.bfloat16),
        in_specs=[pl.BlockSpec(memory_space=pltpu.SMEM)] + [vmem] * (2 + len(chunks)),
        out_specs=vmem,
        compiler_params=pltpu.CompilerParams(vmem_limit_bytes=16 << 20),
        cost_estimate=pl.CostEstimate(
            flops=4 * scored * HD, bytes_accessed=8 << 20, transcendentals=scored
        ),
    )(info, queries, doc_cols, *chunks)


def pin_kernel(x_ref, out_ref):
    out_ref[...] = x_ref[...]


def pin(x):
    return pl.pallas_call(
        pin_kernel,
        out_shape=pltpu.VMEM(x.shape, x.dtype),
        in_specs=[pl.BlockSpec(memory_space=pltpu.VMEM)],
        out_specs=pl.BlockSpec(memory_space=pltpu.VMEM),
        compiler_params=pltpu.CompilerParams(vmem_limit_bytes=4 << 20),
        cost_estimate=pl.CostEstimate(flops=0, bytes_accessed=1 << 10, transcendentals=0),
    )(x)


def swap_blocks(blocks):
    return lax.all_to_all(blocks, "exp", 0, 0, tiled=True)


def norm_kernel(capacity, blocks_ref, out_ref):
    cols = blocks_ref.shape[2]
    rows = [blocks_ref[i].astype(jnp.float32) for i in range(blocks_ref.shape[0])]
    square = sum(
        jnp.sum(r[:capacity] * r[:capacity], axis=1, keepdims=True) for r in rows
    )
    inverse = lax.rsqrt(square / out_ref.shape[1] + NORM_EPS)
    for i, r in enumerate(rows):
        gain = r[capacity : capacity + 1] + (
            r[capacity + 1 : capacity + 2] + r[capacity + 2 : capacity + 3]
        )
        out_ref[:, i * cols : (i + 1) * cols] = (
            r[:capacity] * inverse * gain
        ).astype(jnp.bfloat16)


def normalise(blocks, capacity):
    vmem = pl.BlockSpec(memory_space=pltpu.VMEM)
    count, _, cols = blocks.shape
    return pl.pallas_call(
        functools.partial(norm_kernel, capacity),
        out_shape=jax.ShapeDtypeStruct((capacity, cols * count), jnp.bfloat16),
        in_specs=[vmem],
        out_specs=vmem,
        compiler_params=pltpu.CompilerParams(vmem_limit_bytes=8 << 20),
    )(blocks)


def finish_kernel(core_ref, total_ref, left_ref, back_ref, out_ref):
    count, capacity, cols = out_ref.shape
    whole = jnp.where(
        core_ref[0] == 0, total_ref[:capacity], back_ref[...].astype(jnp.float32)
    ) + left_ref[...].astype(jnp.float32)
    for i in range(count):
        out_ref[i] = whole[:, i * cols : (i + 1) * cols].astype(jnp.bfloat16)


def finish(core, total, left, back, count):
    vmem = pl.BlockSpec(memory_space=pltpu.VMEM)
    capacity, width = left.shape
    return pl.pallas_call(
        finish_kernel,
        out_shape=jax.ShapeDtypeStruct((count, capacity, width // count), jnp.bfloat16),
        in_specs=[pl.BlockSpec(memory_space=pltpu.SMEM)] + [vmem] * 3,
        out_specs=vmem,
        compiler_params=pltpu.CompilerParams(vmem_limit_bytes=8 << 20),
    )(core[None], total, left, back)


def project_kernel(place_ref, heads_ref, *rest):
    blocks, out_ref = rest[:-1], rest[-1]
    heads = heads_ref[...]
    depth = heads.shape[1]
    for i, block in enumerate(blocks):
        rows = slice(block.shape[0] - depth, block.shape[0])
        out_ref[place_ref[i]] = jnp.dot(
            heads, block[rows, :], preferred_element_type=jnp.float32
        ).astype(jnp.bfloat16)


def project(heads_out, found):
    toks, depth = heads_out.shape
    cols = found[0][0].shape[1]
    vmem = pl.BlockSpec(memory_space=pltpu.VMEM)
    return pl.pallas_call(
        project_kernel,
        out_shape=jax.ShapeDtypeStruct((NY * NZ, toks, cols), jnp.bfloat16),
        in_specs=[pl.BlockSpec(memory_space=pltpu.SMEM)] + [vmem] * (1 + len(found)),
        out_specs=vmem,
        compiler_params=pltpu.CompilerParams(vmem_limit_bytes=16 << 20),
        cost_estimate=pl.CostEstimate(
            flops=2 * toks * depth * cols * NY * NZ, bytes_accessed=5 << 20, transcendentals=0
        ),
    )(
        jnp.stack([place for _, place in found]),
        heads_out,
        *[block for block, _ in found],
    )


def per_device(
    hidden_in,
    queries,
    keys,
    values,
    doc_ids,
    out_proj,
    norm_gain,
    routes,
    route_weights,
    w_gate,
    w_up,
    w_down,
):
    tok_rows, slice_width = hidden_in.shape
    experts = lax.axis_size("exp")
    width = slice_width * experts
    ctx_index = lax.axis_index("ctx")
    y, z, k = ctx_index // (NZ * NK), (ctx_index // NK) % NZ, ctx_index % NK
    capacity = min(tok_rows, tok_rows * TOP * 9 // (8 * experts))

    doc_rows = jnp.broadcast_to(
        jnp.concatenate([doc_ids, doc_ids])[None, :].astype(jnp.bfloat16), (16, 2 * HD)
    )
    payload = jnp.concatenate([jnp.concatenate([keys, values], axis=1), doc_rows], axis=0)
    payload, out_proj = together(payload, out_proj)
    kv_shared = share(payload)
    proj_other = send(out_proj, CORE_SWAP)
    proj_block = jnp.concatenate(
        [jnp.where(k == 0, out_proj, proj_other), jnp.where(k == 0, proj_other, out_proj)],
        axis=1,
    )
    chunk = jnp.concatenate(in_order(payload, kv_shared, y, k) + [proj_block], axis=0)
    depth = out_proj.shape[0]

    own_weights = (
        jnp.swapaxes(w_gate[0], 0, 1),
        jnp.swapaxes(w_up[0], 0, 1),
        w_down[0],
    )
    weights = [*load(own_weights), *load([send(w, CORE_SWAP) for w in own_weights])]

    doc_cols = jnp.broadcast_to(doc_ids[:, None].astype(jnp.float32), (tok_rows, HD))
    sign = 2 * k - 1
    hops = NZ // 2
    own_side, other_side = y * NZ, (1 - y) * NZ
    found, chunks, origins = [(chunk, own_side + z)], [chunk], [z]
    across = None
    for step in range(1, hops + 2):
        ahead = (z + sign * (step - 1)) % NZ
        astern = (z - sign * (step - 1)) % NZ
        behind = (z - sign * (step - 2)) % NZ
        sent = [send(chunk[-depth:], PAIR_SWAP)]
        if step <= hops:
            sent.append(send(chunk, RING))
        if 1 < step <= hops:
            sent.append(send(chunk, CORE_SWAP))
        if step > 2:
            sent.append(send(across, CORE_SWAP))
        sent = list(together(*sent))
        across = sent.pop(0)
        found.append((across, other_side + ahead))
        if step > 2:
            found.append((sent.pop(), other_side + behind))
        if 1 < step <= hops:
            swapped = pin(sent.pop())
            found.append((swapped, own_side + astern))
            chunks.append(swapped)
            origins.append(astern)
        if step <= hops:
            chunk = pin(sent.pop())
            ahead = (z + sign * step) % NZ
            found.append((chunk, own_side + ahead))
            chunks.append(chunk)
            origins.append(ahead)
    heads_out = attend(ctx_index, queries, doc_cols, chunks, origins)

    part = project(heads_out, found)
    part = part.reshape(experts, NY * NZ // experts * tok_rows, -1)
    summed = jnp.sum(swap_blocks(part).astype(jnp.float32), axis=0)
    summed = summed.reshape(-1, tok_rows, summed.shape[1])
    attn_slice = jnp.concatenate([summed[i] for i in range(summed.shape[0])], axis=1)
    resid = (hidden_in.astype(jnp.float32) + attn_slice).astype(jnp.bfloat16)

    expert_ids = jnp.arange(experts, dtype=jnp.int32)
    matches = routes[:, :, None] == expert_ids
    hit_counts = jnp.sum(matches.astype(jnp.int32), axis=1)
    slot_rank = jnp.cumsum(hit_counts, axis=0, dtype=jnp.int32) - 1
    slot_ids = jnp.arange(capacity, dtype=jnp.int32)
    placed_slots = (slot_rank[:, :, None] == slot_ids) & (hit_counts[:, :, None] > 0)
    picked = jnp.einsum(
        "tec,td->ecd",
        placed_slots.astype(jnp.bfloat16),
        resid,
        preferred_element_type=jnp.float32,
    ).astype(jnp.bfloat16)
    high = lax.reduce_precision(norm_gain, 8, 7)
    middle = lax.reduce_precision(norm_gain - high, 8, 7)
    low = norm_gain - high - middle
    gain_rows = jnp.stack([high, middle, low, jnp.zeros_like(low)]).astype(jnp.bfloat16)
    picked = jnp.concatenate(
        [picked, jnp.broadcast_to(gain_rows, (experts, *gain_rows.shape))], axis=1
    )
    rows = normalise(swap_blocks(picked), capacity)

    entered = send(rows, ENTER)
    crossed = send(rows, ENTER_SECOND)
    chunk = jnp.concatenate(
        [jnp.where(k == 0, rows, entered), jnp.where(k == 0, entered, crossed)], axis=0
    )
    chunks = [chunk]
    for step in range(1, NZ):
        near = step <= NZ // 2
        chunks.append(
            send(chunks[-1], RING) if near else send(chunks[NZ - step], CROSS_SWAP)
        )
    running = None
    for step in range(1, NZ):
        part = expert_partial(chunks[step], weights)
        if step > 1:
            part = send(running, RING).astype(jnp.float32) + part
        running = part.astype(jnp.bfloat16)
    part = expert_partial(chunks[0], weights)
    total = send(running, RING).astype(jnp.float32) + part

    leaving = jnp.where(k == 0, total[capacity:], total[:capacity]).astype(jnp.bfloat16)
    left = send(leaving, LEAVE)
    back = send(total[capacity:].astype(jnp.bfloat16), ENTER_SECOND)

    expert_out = swap_blocks(finish(k, total, left, back, experts))
    weight_map = jnp.sum(jnp.where(matches, route_weights[:, :, None], 0.0), axis=1)
    combine = (weight_map[:, :, None] * placed_slots.astype(jnp.float32)).reshape(
        tok_rows, experts * capacity
    )
    expert_flat = expert_out.reshape(experts * capacity, slice_width).astype(jnp.float32)
    expert_mix = jnp.dot(combine, expert_flat, precision=lax.Precision.HIGHEST)
    return (resid.astype(jnp.float32) + expert_mix).astype(jnp.bfloat16)


def solution(mesh):
    in_specs = (
        P("ctx", "exp"),
        P("ctx", "exp"),
        P("ctx", "exp"),
        P("ctx", "exp"),
        P("ctx"),
        P("exp", "ctx"),
        P("exp"),
        P("ctx", None),
        P("ctx", None),
        P("exp", None, "ctx"),
        P("exp", None, "ctx"),
        P("exp", "ctx", None),
    )
    out_specs = P("ctx", "exp")
    return jax.shard_map(
        per_device, mesh=mesh, in_specs=in_specs, out_specs=out_specs, check_vma=False
    )
```
